32 devices in a mesh: groups: 2 (over y), tiles: 4 (over z), rows: 2 (over x), tok: 2 (over core).
Axes of the slice: x: 2, y: 2, z: 4, core: 2. Of those that a mesh axis runs over, the one named last changes fastest.
Arguments:
- x_act: bfloat16 [2, 1536, 8192], P('tok', 'groups', 'rows'), parts along dimension 1, may hold values from -6 to 6
- grad_out: bfloat16 [2, 1536, 28672], P('tok', 'groups', ('tiles', 'rows')), parts along dimension 1, may hold values from -0.21875 to 0.21875
- surv_rows: int32 [8, 2, 64], P(('groups', 'tiles'), 'rows'), parts along dimension 0, may hold values from 0 to 31, as said below
- surv_cols: int32 [8, 2, 64], P(('groups', 'tiles'), 'rows'), parts along dimension 0, may hold values from 0 to 55, as said below
- counts: int32 [8, 2], P(('groups', 'tiles'), 'rows'), parts along dimension 0, may hold values from 16 to 64, as said below
Outputs:
- fisher: float32 [8, 2, 64, 128, 128], P(('groups', 'tiles'), 'rows', None, 'tok'), parts along dimension 0
The draws below stay inside these ranges and needn't reach their ends.
There are 2 independent parts, one for each index of `groups`. The reference program is written for one: setup_inputs(seed, part) draws one part's arguments, and reference() takes and returns one part's arrays. A program takes and returns all parts, laid end to end along the dimension named above; each array names one. Nothing has to cross between parts.
Inputs may be any that keep to these rules, and one draw needn't show every extreme that they name: `surv_rows`: the (row tile, column tile) pairs listed in one device's slots are distinct. `surv_cols`: same slots as surv_rows. A device's survivors occupy its slots 0 to counts - 1; in every draw some device lists 64.
All inputs are finite; a program needn't handle non-finite values.
Results may differ from the reference program's by a relative error of at most 0.0003.
Values may be sent and summed in bfloat16 or wider, within the bound.
A program may use at most 128 MiB of HBM per device.

```python
import jax
import jax.numpy as jnp
from jax import lax

D = 8192
F = 28672
TILE = 128
TOK = 768
CAP = 64
SAMPLES = 2
RT_DEV = 32
CT_DEV = 56
N_TILES = 4
N_ROWS = 2


def remaining_tiles(key):
    row_tiles = D // TILE // N_ROWS
    col_tiles = F // TILE // N_TILES
    block_tiles = row_tiles * col_tiles
    list_key_array = jax.random.split(key, N_TILES * N_ROWS)

    def one_list(list_key):
        shuffled = jax.random.permutation(list_key, block_tiles)
        return shuffled[:CAP].astype(jnp.int32)
    chosen = jax.vmap(one_list)(list_key_array).reshape(N_TILES, N_ROWS, CAP)
    return (chosen // col_tiles, chosen % col_tiles)


def draw_surv_rows(key, part):
    return remaining_tiles(key)[0]


def draw_surv_cols(key, part):
    return remaining_tiles(key)[1]


def draw_counts(key, part):
    key = jax.random.fold_in(key, 7)
    base_key, heavy_key, pick_key = jax.random.split(key, 3)
    base_load = jax.random.randint(base_key, (N_TILES, N_ROWS), CAP // 4, CAP + 1)
    largest_load = jax.random.randint(heavy_key, (N_TILES, N_ROWS), 3 * CAP // 4, CAP + 1)
    largest_total = max(1, N_TILES // 4)
    ranking = jax.random.permutation(pick_key, N_TILES).astype(jnp.int32)
    on_heavy = (ranking < largest_total)[:, None]
    loads = jnp.where(on_heavy, largest_load, base_load)
    top_row = (ranking == 0)[:, None] & (jnp.arange(N_ROWS, dtype=jnp.int32)[None, :] == 0)
    return jnp.where(top_row, CAP, loads).astype(jnp.int32)


def levels(stream_key, extent, cuts, low, largest):
    factor_of = 1.0
    for dim, shards_of in cuts:
        steps = jax.random.uniform(jax.random.fold_in(jax.random.fold_in(stream_key, 6), dim), (shards_of,), jnp.float32, low / len(cuts), largest / len(cuts))
        factor_of = factor_of * jnp.repeat(jnp.exp(steps), extent[dim] // shards_of).reshape((-1,) + (1,) * (len(extent) - 1 - dim))
    return factor_of


def bell_draw(rng, dims, width, bound, cuts=(), held_as=jnp.bfloat16):
    values = width * jax.random.normal(rng, dims, jnp.float32)
    if cuts:
        values = values * levels(rng, dims, cuts, -0.22, 0.18)
    return jnp.clip(values, -bound, bound).astype(held_as)


def setup_inputs(seed: int = 0, part: int = 0) -> dict:
    key_of = jax.random.split(jax.random.key(seed), 6)
    part_splits = jax.random.split(jax.random.fold_in(key_of[5], part), 6)
    x_act = bell_draw(part_splits[0], (SAMPLES, TOK, D), 1.0, 6.0, ((0, 2), (2, 2)))
    grad_out = bell_draw(part_splits[1], (SAMPLES, TOK, F), TOK ** -0.5, 0.21875, ((0, 2), (2, 8)))
    surv_rows = draw_surv_rows(jax.random.fold_in(jax.random.fold_in(key_of[5], part), 71), part)
    surv_cols = draw_surv_cols(jax.random.fold_in(jax.random.fold_in(key_of[5], part), 71), part)
    counts = draw_counts(jax.random.fold_in(jax.random.fold_in(key_of[5], part), 71), part)
    return dict(x_act=x_act, grad_out=grad_out, surv_rows=surv_rows, surv_cols=surv_cols, counts=counts)


def reference(x_act, grad_out, surv_rows, surv_cols, counts):
    sample_count = x_act.shape[0]
    x_tiles = x_act.astype(jnp.float32).reshape(sample_count, TOK, D // TILE, TILE)
    y_tiles = grad_out.astype(jnp.float32).reshape(sample_count, TOK, F // TILE, TILE)
    tiles_index = jnp.arange(N_TILES, dtype=jnp.int32)[:, None, None]
    rows_index = jnp.arange(N_ROWS, dtype=jnp.int32)[None, :, None]
    global_rows = (surv_rows + rows_index * RT_DEV).astype(jnp.int32).reshape(N_TILES * N_ROWS, CAP)
    global_cols = (surv_cols + tiles_index * CT_DEV).astype(jnp.int32).reshape(N_TILES * N_ROWS, CAP)
    slot_live = (jnp.arange(CAP, dtype=jnp.int32)[None, None, :] < counts[:, :, None]).reshape(N_TILES * N_ROWS, CAP)

    def owner_tiles(inputs):
        row_ids, col_ids, is_live = inputs
        x_panels = jnp.take(x_tiles, row_ids, axis=2)
        y_panels = jnp.take(y_tiles, col_ids, axis=2)
        gradients = jnp.einsum("stck,stcj->sckj", x_panels, y_panels, precision=lax.Precision.HIGHEST)
        squared = jnp.sum(gradients * gradients, axis=0)
        return jnp.where(is_live[:, None, None], squared, jnp.zeros_like(squared))

    result = lax.map(owner_tiles, (global_rows, global_cols, slot_live))
    return result.reshape(N_TILES, N_ROWS, CAP, TILE, TILE)
```

```python
import functools

import jax
import jax.numpy as jnp
from jax import lax
from jax.experimental import pallas as pl
from jax.experimental.pallas import tpu as pltpu
from jax.sharding import PartitionSpec as P

TILE = 128


def square_tiles(x_tiles, panel_fetch, row_index, live_count, places, slot_total):
    tile_extent = x_tiles.shape[2]
    block_size = min(16, slot_total)
    result = jnp.zeros((slot_total, tile_extent, tile_extent), jnp.float32)

    def one_block(block_index, totals):
        first_slot = block_index * block_size
        rows_here = lax.dynamic_slice_in_dim(row_index, first_slot, block_size)
        x_panels = jnp.take(x_tiles, rows_here, axis=1)
        y_panels = panel_fetch(first_slot, block_size)
        gradients = jnp.einsum(
            "tnk,tnj->nkj", x_panels, y_panels, preferred_element_type=jnp.float32
        )
        is_live = first_slot + jnp.arange(block_size, dtype=jnp.int32) < live_count
        squares = jnp.where(is_live[:, None, None], gradients * gradients, 0.0)
        where_to = lax.dynamic_slice_in_dim(places, first_slot, block_size)
        return totals.at[where_to].set(squares)

    trip_count = (live_count + block_size - 1) // block_size
    return lax.fori_loop(0, trip_count, one_block, result)


def sum_samples(partial_value):
    return lax.psum_scatter(partial_value, "tok", scatter_dimension=1, tiled=True)


def on_device(x_act, grad_out, surv_rows, surv_cols, counts):
    tile_extent = TILE
    gathered = lax.all_gather(grad_out, "rows", axis=2, tiled=True)
    length_value = x_act.shape[1]
    x_tiles = x_act[0].reshape(length_value, -1, tile_extent)
    y_tiles = gathered[0].reshape(length_value, -1, tile_extent)
    row_listing = surv_rows[0, 0]
    cols_list = surv_cols[0, 0]
    live_here = counts[0, 0]
    capacity = row_listing.shape[0]
    keep_count = capacity // 2

    def from_own(first_slot, block_size):
        cols_here = lax.dynamic_slice_in_dim(cols_list, first_slot, block_size)
        return jnp.take(y_tiles, cols_here, axis=1)

    owners = lax.axis_size("tiles")
    position = lax.axis_index("tiles")
    deal_size = (capacity - keep_count) // owners
    own_places = jnp.arange(keep_count, dtype=jnp.int32)
    own_part = square_tiles(
        x_tiles,
        from_own,
        row_listing[:keep_count],
        jnp.minimum(live_here, keep_count),
        own_places,
        keep_count,
    )
    outbound_tiles = jnp.take(y_tiles, cols_list[keep_count:], axis=1)
    outbound_tiles = outbound_tiles.reshape(length_value, owners, deal_size, tile_extent)
    outbound_tiles = jnp.roll(outbound_tiles, position, axis=1).reshape(
        length_value, owners * deal_size, tile_extent
    )
    incoming = lax.all_to_all(outbound_tiles, "tiles", split_axis=1, concat_axis=1, tiled=True)
    all_rows, all_counts = (
        lax.all_gather(surv_rows, "tiles", axis=0, tiled=True),
        lax.all_gather(counts, "tiles", axis=0, tiled=True),
    )
    sources = jnp.arange(owners, dtype=jnp.int32)
    block_of = (position - sources) % owners
    slot_ids = (
        keep_count + block_of[:, None] * deal_size + jnp.arange(deal_size, dtype=jnp.int32)[None, :]
    )
    wanted_rows = jnp.take_along_axis(all_rows[:, 0, :], slot_ids, axis=1).reshape(-1)
    is_wanted = (slot_ids < all_counts[:, 0][:, None]).reshape(-1)
    ordering = jnp.argsort(1 - is_wanted.astype(jnp.int32), stable=True)
    wanted_total = jnp.sum(is_wanted.astype(jnp.int32))

    def from_incoming(first_slot, block_size):
        picks = lax.dynamic_slice_in_dim(ordering, first_slot, block_size)
        return jnp.take(incoming, picks, axis=1)

    helped = square_tiles(
        x_tiles, from_incoming, wanted_rows[ordering], wanted_total, ordering, owners * deal_size
    )
    returned_tiles = lax.all_to_all(helped, "tiles", split_axis=0, concat_axis=0, tiled=True)
    returned_tiles = returned_tiles.reshape(owners, deal_size, tile_extent, tile_extent)
    returned_tiles = jnp.roll(returned_tiles, -position, axis=0).reshape(
        owners * deal_size, tile_extent, tile_extent
    )
    fisher = sum_samples(jnp.concatenate([own_part, returned_tiles], axis=0))
    return fisher[None, None]


def pack_body(pick_ref, y_ref, out_ref):
    out_ref[...] = y_ref[...]


def pack_panels(y, picks):
    tokens = y.shape[1]
    chosen = picks.shape[0]
    return pl.pallas_call(
        pack_body,
        out_shape=jax.ShapeDtypeStruct((chosen, tokens, TILE), y.dtype),
        grid_spec=pltpu.PrefetchScalarGridSpec(
            num_scalar_prefetch=1,
            grid=(chosen,),
            in_specs=[pl.BlockSpec((1, tokens, TILE), lambda i, p: (0, 0, p[i]))],
            out_specs=pl.BlockSpec((1, tokens, TILE), lambda i, p: (i, 0, 0)),
        ),
        cost_estimate=pl.CostEstimate(
            flops=0, bytes_accessed=4 * chosen * tokens * TILE, transcendentals=0
        ),
        name="pack_panels",
    )(picks, y)


def square_body(apart, steps_ref, rows_ref, cols_ref, slots_ref, x_ref, y_ref, a_ref, b_ref, keep_ref, send_ref):
    del a_ref, b_ref
    tokens = x_ref.shape[1]
    half = TILE // 2
    first = lax.axis_index("tok") == 0

    def one_slot(x_tile, y_tile, keep_tile, send_tile):
        gradient = lax.dot_general(
            x_tile[0], y_tile[0], (((0,), (0,)), ((), ())), preferred_element_type=jnp.float32
        )
        squares = gradient * gradient

        @pl.when(first)
        def _():
            keep_tile[0] = squares[:half]
            send_tile[0] = squares[half:]

        @pl.when(jnp.logical_not(first))
        def _():
            keep_tile[0] = squares[half:]
            send_tile[0] = squares[:half]

    y_map = (lambda i: (cols_ref[i], 0, 0)) if apart else (lambda i: (0, 0, cols_ref[i]))
    out_spec = pl.BlockSpec((1, half, TILE), lambda i: (slots_ref[i], 0, 0))
    pltpu.emit_pipeline(
        one_slot,
        grid=(steps_ref[0],),
        in_specs=[
            pl.BlockSpec((1, tokens, TILE), lambda i: (0, 0, rows_ref[i])),
            pl.BlockSpec((1, tokens, TILE), y_map),
        ],
        out_specs=[out_spec, out_spec],
    )(x_ref, y_ref, keep_ref, send_ref)


def square_slots(x, y, steps, rows, cols, slots, keep, send, panels_apart):
    tokens = x.shape[1]
    any_spec = pl.BlockSpec(memory_space=pl.ANY)
    smem_spec = pl.BlockSpec(memory_space=pltpu.SMEM)
    expected = max(1, rows.shape[0] // (8 if panels_apart else 2))
    return pl.pallas_call(
        functools.partial(square_body, panels_apart),
        out_shape=(
            jax.ShapeDtypeStruct(keep.shape, keep.dtype),
            jax.ShapeDtypeStruct(send.shape, send.dtype),
        ),
        in_specs=[smem_spec] * 4 + [any_spec] * 4,
        out_specs=(any_spec, any_spec),
        input_output_aliases={6: 0, 7: 1},
        cost_estimate=pl.CostEstimate(
            flops=expected * 2 * tokens * TILE * TILE,
            bytes_accessed=expected * (4 * tokens * TILE + 4 * TILE * TILE),
            transcendentals=0,
        ),
        name="square_slots",
    )(steps.reshape(1), rows, cols, slots, x, y, keep, send)


def chunk_sizes(total):
    last = max(1, total // 8)
    rest = total - last
    parts = 3
    sizes = [rest // parts + (1 if i < rest % parts else 0) for i in range(parts)]
    return sizes + [last]


def exchange_and_square(total, operands):
    x, y, picks, keys, rows, cols, slots, keep, send = operands
    sizes = chunk_sizes(total)
    swap = [(0, 1), (1, 0)]
    arrived = []
    first = 0
    for size in sizes:
        packed = pack_panels(y, picks[first : first + size])
        arrived.append(lax.ppermute(packed, "rows", swap))
        first += size
    capacity = rows.shape[0]
    dummy = keep.shape[0] - 1

    def phase(panels, low, high, keep, send, apart):
        begin = jnp.sum((keys < low).astype(jnp.int32))
        steps = jnp.sum((keys < high).astype(jnp.int32)) - begin
        live = steps > 0
        roll = lambda v: lax.dynamic_slice(jnp.concatenate([v, v]), (begin,), (capacity,))
        here_cols = roll(cols) - (low if apart else 0)
        here_cols = jnp.where(live, here_cols, 0)
        here_cols = jnp.clip(here_cols, 0, (high - low - 1) if apart else y.shape[2] // TILE - 1)
        here_slots = jnp.where(live, roll(slots), dummy)
        return square_slots(
            x, panels, jnp.maximum(steps, 1), roll(rows), here_cols, here_slots, keep, send, apart
        )

    keep, send = phase(y, -1, 0, keep, send, False)
    first = 0
    for size, panels in zip(sizes, arrived):
        keep, send = phase(panels, first, first + size, keep, send, True)
        first += size
    return keep, send


def on_pair(x_act, grad_out, surv_rows, surv_cols, counts):
    own_tiles = grad_out.shape[2] // TILE
    capacity = surv_rows.shape[2]
    row_place = lax.axis_index("rows")
    slot_ids = jnp.arange(capacity, dtype=jnp.int32)
    live = slot_ids < counts[0, 0]
    listed = jnp.where(live, surv_cols[0, 0], -1)
    axes = ("groups", "tiles", "rows")
    everyone = lax.all_gather(listed, axes, axis=0, tiled=False)
    columns = jnp.arange(2 * own_tiles, dtype=jnp.int32)
    needed = jnp.any(everyone[:, None, :] == columns[None, :, None], axis=2)
    owner_rows = (jnp.arange(everyone.shape[0], dtype=jnp.int32) % 2)[:, None]
    remote = needed & ((columns // own_tiles)[None, :] != owner_rows)
    largest = jnp.max(jnp.sum(remote.astype(jnp.int32), axis=1))

    me = (lax.axis_index("groups") * lax.axis_size("tiles") + lax.axis_index("tiles")) * 2 + row_place

    def places(owner, holder):
        wanted = lax.dynamic_slice(remote, (owner, holder * own_tiles), (1, own_tiles))[0]
        wanted = wanted.astype(jnp.int32)
        ids = jnp.arange(own_tiles, dtype=jnp.int32)
        before = jnp.sum(jnp.where(ids[None, :] < ids[:, None], wanted[None, :], 0), axis=1)
        return wanted, before

    ids = jnp.arange(own_tiles, dtype=jnp.int32)
    partner = me + 1 - 2 * row_place
    wanted, before = places(partner, row_place)
    picks = jnp.sum(
        jnp.where((wanted[None, :] > 0) & (before[None, :] == ids[:, None]), ids[None, :], 0), axis=1
    )
    _, arrival = places(me, 1 - row_place)
    within = listed % own_tiles
    is_local = listed // own_tiles == row_place
    place = jnp.sum(jnp.where(within[:, None] == ids[None, :], arrival[None, :], 0), axis=1)
    key = jnp.where(live, jnp.where(is_local, -1, place), 2 * own_tiles)
    ahead = (key[None, :] < key[:, None]) | (
        (key[None, :] == key[:, None]) & (slot_ids[None, :] < slot_ids[:, None])
    )
    rank = jnp.sum(ahead.astype(jnp.int32), axis=1)
    chosen = rank[None, :] == slot_ids[:, None]
    ordered = lambda v: jnp.sum(jnp.where(chosen, v[None, :], 0), axis=1)
    keys = ordered(key)
    rows = ordered(surv_rows[0, 0])
    cols = ordered(jnp.where(is_local, within, place))
    slots = ordered(slot_ids)

    half = TILE // 2
    keep = jnp.zeros((capacity + 1, half, TILE), jnp.float32)
    send = jnp.zeros((capacity + 1, half, TILE), jnp.float32)
    totals = sorted({max(4, own_tiles * n // 28) for n in TOTALS} | {own_tiles})
    branch = jnp.sum((largest > jnp.array(totals[:-1], jnp.int32)).astype(jnp.int32))
    operands = (x_act, grad_out, picks, keys, rows, cols, slots, keep, send)
    keep, send = lax.switch(
        branch, [functools.partial(exchange_and_square, total) for total in totals], operands
    )
    other = lax.ppermute(send, "tok", [(0, 1), (1, 0)])
    return (keep + other)[:capacity][None, None]


TOTALS = (12, 16, 18, 20, 22, 24, 28)


def solution(mesh):
    return functools.partial(choose, mesh)


def choose(mesh, x_act, grad_out, surv_rows, surv_cols, counts):
    own_columns = grad_out.shape[2] // (mesh.shape["tiles"] * mesh.shape["rows"])
    paired = (
        mesh.shape["rows"] == 2
        and mesh.shape["tok"] == 2
        and own_columns % TILE == 0
        and own_columns // TILE >= 4
    )
    return spread(mesh, on_pair if paired else on_device)(
        x_act, grad_out, surv_rows, surv_cols, counts
    )


def spread(mesh, body):
    return jax.shard_map(
        body,
        mesh=mesh,
        in_specs=(
            P("tok", "groups", "rows"),
            P("tok", "groups", ("tiles", "rows")),
            P(("groups", "tiles"), "rows", None),
            P(("groups", "tiles"), "rows", None),
            P(("groups", "tiles"), "rows"),
        ),
        out_specs=P(("groups", "tiles"), "rows", None, "tok", None),
        check_vma=False,
    )
```

```python
import functools

import jax
import jax.numpy as jnp
from jax import lax
from jax.experimental import pallas as pl
from jax.experimental.pallas import tpu as pltpu
from jax.sharding import PartitionSpec as P

TILE = 128


def square_tiles(x_tiles, panel_fetch, row_index, live_count, places, slot_total):
    tile_extent = x_tiles.shape[2]
    block_size = min(16, slot_total)
    result = jnp.zeros((slot_total, tile_extent, tile_extent), jnp.float32)

    def one_block(block_index, totals):
        first_slot = block_index * block_size
        rows_here = lax.dynamic_slice_in_dim(row_index, first_slot, block_size)
        x_panels = jnp.take(x_tiles, rows_here, axis=1)
        y_panels = panel_fetch(first_slot, block_size)
        gradients = jnp.einsum(
            "tnk,tnj->nkj", x_panels, y_panels, preferred_element_type=jnp.float32
        )
        is_live = first_slot + jnp.arange(block_size, dtype=jnp.int32) < live_count
        squares = jnp.where(is_live[:, None, None], gradients * gradients, 0.0)
        where_to = lax.dynamic_slice_in_dim(places, first_slot, block_size)
        return totals.at[where_to].set(squares)

    trip_count = (live_count + block_size - 1) // block_size
    return lax.fori_loop(0, trip_count, one_block, result)


def sum_samples(partial_value):
    return lax.psum_scatter(partial_value, "tok", scatter_dimension=1, tiled=True)


def on_device(x_act, grad_out, surv_rows, surv_cols, counts):
    tile_extent = TILE
    gathered = lax.all_gather(grad_out, "rows", axis=2, tiled=True)
    length_value = x_act.shape[1]
    x_tiles = x_act[0].reshape(length_value, -1, tile_extent)
    y_tiles = gathered[0].reshape(length_value, -1, tile_extent)
    row_listing = surv_rows[0, 0]
    cols_list = surv_cols[0, 0]
    live_here = counts[0, 0]
    capacity = row_listing.shape[0]
    keep_count = capacity // 2

    def from_own(first_slot, block_size):
        cols_here = lax.dynamic_slice_in_dim(cols_list, first_slot, block_size)
        return jnp.take(y_tiles, cols_here, axis=1)

    owners = lax.axis_size("tiles")
    position = lax.axis_index("tiles")
    deal_size = (capacity - keep_count) // owners
    own_places = jnp.arange(keep_count, dtype=jnp.int32)
    own_part = square_tiles(
        x_tiles,
        from_own,
        row_listing[:keep_count],
        jnp.minimum(live_here, keep_count),
        own_places,
        keep_count,
    )
    outbound_tiles = jnp.take(y_tiles, cols_list[keep_count:], axis=1)
    outbound_tiles = outbound_tiles.reshape(length_value, owners, deal_size, tile_extent)
    outbound_tiles = jnp.roll(outbound_tiles, position, axis=1).reshape(
        length_value, owners * deal_size, tile_extent
    )
    incoming = lax.all_to_all(outbound_tiles, "tiles", split_axis=1, concat_axis=1, tiled=True)
    all_rows, all_counts = (
        lax.all_gather(surv_rows, "tiles", axis=0, tiled=True),
        lax.all_gather(counts, "tiles", axis=0, tiled=True),
    )
    sources = jnp.arange(owners, dtype=jnp.int32)
    block_of = (position - sources) % owners
    slot_ids = (
        keep_count + block_of[:, None] * deal_size + jnp.arange(deal_size, dtype=jnp.int32)[None, :]
    )
    wanted_rows = jnp.take_along_axis(all_rows[:, 0, :], slot_ids, axis=1).reshape(-1)
    is_wanted = (slot_ids < all_counts[:, 0][:, None]).reshape(-1)
    ordering = jnp.argsort(1 - is_wanted.astype(jnp.int32), stable=True)
    wanted_total = jnp.sum(is_wanted.astype(jnp.int32))

    def from_incoming(first_slot, block_size):
        picks = lax.dynamic_slice_in_dim(ordering, first_slot, block_size)
        return jnp.take(incoming, picks, axis=1)

    helped = square_tiles(
        x_tiles, from_incoming, wanted_rows[ordering], wanted_total, ordering, owners * deal_size
    )
    returned_tiles = lax.all_to_all(helped, "tiles", split_axis=0, concat_axis=0, tiled=True)
    returned_tiles = returned_tiles.reshape(owners, deal_size, tile_extent, tile_extent)
    returned_tiles = jnp.roll(returned_tiles, -position, axis=0).reshape(
        owners * deal_size, tile_extent, tile_extent
    )
    fisher = sum_samples(jnp.concatenate([own_part, returned_tiles], axis=0))
    return fisher[None, None]


def share_body(listed_ref, all_ref, send_sems, recv_sems, own_sem):
    tiles, row_count = lax.axis_size("tiles"), lax.axis_size("rows")
    owners = all_ref.shape[0]
    me = (
        lax.axis_index("groups") * tiles + lax.axis_index("tiles")
    ) * row_count + lax.axis_index("rows")

    def peer(step):
        there = lax.rem(me + step, owners)
        return {
            "groups": there // (tiles * row_count),
            "tiles": lax.rem(there // row_count, tiles),
            "rows": lax.rem(there, row_count),
        }

    barrier = pltpu.get_barrier_semaphore()
    for step in range(1, owners):
        pl.semaphore_signal(
            barrier, inc=1, device_id=peer(step), device_id_type=pl.DeviceIdType.MESH
        )
    pl.semaphore_wait(barrier, owners - 1)
    own = pltpu.make_async_copy(listed_ref, all_ref.at[me], own_sem)
    own.start()
    copies = []
    for step in range(1, owners):
        copy = pltpu.make_async_remote_copy(
            src_ref=listed_ref,
            dst_ref=all_ref.at[me],
            send_sem=send_sems.at[step],
            recv_sem=recv_sems.at[step],
            device_id=peer(step),
            device_id_type=pl.DeviceIdType.MESH,
        )
        copy.start()
        copies.append(copy)
    own.wait()
    for copy in copies:
        copy.wait()


def share_lists(listed):
    owners = lax.axis_size("groups") * lax.axis_size("tiles") * lax.axis_size("rows")
    capacity = listed.shape[0]
    lanes = -(-capacity // 128) * 128
    row = jnp.broadcast_to(jnp.pad(listed, (0, lanes - capacity))[None, :], (8, lanes))
    shared = pl.pallas_call(
        share_body,
        out_shape=jax.ShapeDtypeStruct((owners, 8, lanes), jnp.int32),
        in_specs=[pl.BlockSpec(memory_space=pltpu.VMEM)],
        out_specs=pl.BlockSpec(memory_space=pltpu.VMEM),
        scratch_shapes=[
            pltpu.SemaphoreType.DMA((owners,)),
            pltpu.SemaphoreType.DMA((owners,)),
            pltpu.SemaphoreType.DMA,
        ],
        compiler_params=pltpu.CompilerParams(collective_id=3, has_side_effects=True),
        name="share_lists",
    )(row)
    return shared[:, 0, :capacity]


def pack_body(pick_ref, y_ref, out_ref, sems):
    copies = []
    for i in range(out_ref.shape[0]):
        first = pl.multiple_of(pick_ref[i] * TILE, TILE)
        copy = pltpu.make_async_copy(
            y_ref.at[0, :, pl.ds(first, TILE)], out_ref.at[i], sems.at[i]
        )
        copy.start()
        copies.append(copy)
    for copy in copies:
        copy.wait()


def pack_panels(y, picks):
    tokens = y.shape[1]
    chosen = picks.shape[0]
    return pl.pallas_call(
        pack_body,
        out_shape=jax.ShapeDtypeStruct((chosen, tokens, TILE), y.dtype),
        in_specs=[pl.BlockSpec(memory_space=pltpu.SMEM), pl.BlockSpec(memory_space=pl.ANY)],
        out_specs=pl.BlockSpec(memory_space=pl.ANY),
        scratch_shapes=[pltpu.SemaphoreType.DMA((chosen,))],
        cost_estimate=pl.CostEstimate(
            flops=0, bytes_accessed=4 * chosen * tokens * TILE, transcendentals=0
        ),
        name="pack_panels",
    )(picks, y)


def square_body(apart, steps_ref, rows_ref, cols_ref, slots_ref, x_ref, y_ref, a_ref, b_ref, keep_ref, send_ref):
    del a_ref, b_ref
    tokens = x_ref.shape[1]
    half = TILE // 2
    first = lax.axis_index("tok") == 0

    def one_slot(x_tile, y_tile, keep_tile, send_tile):
        gradient = lax.dot_general(
            x_tile[0], y_tile[0], (((0,), (0,)), ((), ())), preferred_element_type=jnp.float32
        )
        squares = gradient * gradient

        @pl.when(first)
        def _():
            keep_tile[0] = squares[:half]
            send_tile[0] = squares[half:]

        @pl.when(jnp.logical_not(first))
        def _():
            keep_tile[0] = squares[half:]
            send_tile[0] = squares[:half]

    y_map = (lambda i: (cols_ref[i], 0, 0)) if apart else (lambda i: (0, 0, cols_ref[i]))
    out_spec = pl.BlockSpec((1, half, TILE), lambda i: (slots_ref[i], 0, 0))
    pltpu.emit_pipeline(
        one_slot,
        grid=(steps_ref[0],),
        in_specs=[
            pl.BlockSpec((1, tokens, TILE), lambda i: (0, 0, rows_ref[i])),
            pl.BlockSpec((1, tokens, TILE), y_map),
        ],
        out_specs=[out_spec, out_spec],
    )(x_ref, y_ref, keep_ref, send_ref)


def square_slots(x, y, steps, rows, cols, slots, keep, send, panels_apart):
    tokens = x.shape[1]
    any_spec = pl.BlockSpec(memory_space=pl.ANY)
    smem_spec = pl.BlockSpec(memory_space=pltpu.SMEM)
    expected = max(1, rows.shape[0] // (8 if panels_apart else 2))
    return pl.pallas_call(
        functools.partial(square_body, panels_apart),
        out_shape=(
            jax.ShapeDtypeStruct(keep.shape, keep.dtype),
            jax.ShapeDtypeStruct(send.shape, send.dtype),
        ),
        in_specs=[smem_spec] * 4 + [any_spec] * 4,
        out_specs=(any_spec, any_spec),
        input_output_aliases={6: 0, 7: 1},
        cost_estimate=pl.CostEstimate(
            flops=expected * 2 * tokens * TILE * TILE,
            bytes_accessed=expected * (4 * tokens * TILE + 4 * TILE * TILE),
            transcendentals=0,
        ),
        name="square_slots",
    )(steps.reshape(1), rows, cols, slots, x, y, keep, send)


def chunk_sizes(total):
    last = max(1, total // 8)
    rest = total - last
    parts = 3
    sizes = [rest // parts + (1 if i < rest % parts else 0) for i in range(parts)]
    return sizes + [last]


def exchange_and_square(total, operands):
    x, y, picks, keys, rows, cols, slots, keep, send = operands
    sizes = chunk_sizes(total)
    swap = [(0, 1), (1, 0)]
    arrived = []
    first = 0
    for size in sizes:
        packed = pack_panels(y, picks[first : first + size])
        arrived.append(lax.ppermute(packed, "rows", swap))
        first += size
    capacity = rows.shape[0]
    dummy = keep.shape[0] - 1

    def phase(panels, low, high, keep, send, apart):
        begin = jnp.sum((keys < low).astype(jnp.int32))
        steps = jnp.sum((keys < high).astype(jnp.int32)) - begin
        live = steps > 0
        roll = lambda v: lax.dynamic_slice(jnp.concatenate([v, v]), (begin,), (capacity,))
        here_cols = roll(cols) - (low if apart else 0)
        here_cols = jnp.where(live, here_cols, 0)
        here_cols = jnp.clip(here_cols, 0, (high - low - 1) if apart else y.shape[2] // TILE - 1)
        here_slots = jnp.where(live, roll(slots), dummy)
        return square_slots(
            x, panels, jnp.maximum(steps, 1), roll(rows), here_cols, here_slots, keep, send, apart
        )

    keep, send = phase(y, -1, 0, keep, send, False)
    first = 0
    for size, panels in zip(sizes, arrived):
        keep, send = phase(panels, first, first + size, keep, send, True)
        first += size
    return keep, send


def on_pair(x_act, grad_out, surv_rows, surv_cols, counts):
    own_tiles = grad_out.shape[2] // TILE
    capacity = surv_rows.shape[2]
    row_place = lax.axis_index("rows")
    slot_ids = jnp.arange(capacity, dtype=jnp.int32)
    live = slot_ids < counts[0, 0]
    listed = jnp.where(live, surv_cols[0, 0], -1)
    everyone = share_lists(listed)
    columns = jnp.arange(2 * own_tiles, dtype=jnp.int32)
    needed = jnp.any(everyone[:, None, :] == columns[None, :, None], axis=2)
    owner_rows = (jnp.arange(everyone.shape[0], dtype=jnp.int32) % 2)[:, None]
    remote = needed & ((columns // own_tiles)[None, :] != owner_rows)
    largest = jnp.max(jnp.sum(remote.astype(jnp.int32), axis=1))

    me = (lax.axis_index("groups") * lax.axis_size("tiles") + lax.axis_index("tiles")) * 2 + row_place

    def places(owner, holder):
        wanted = lax.dynamic_slice(remote, (owner, holder * own_tiles), (1, own_tiles))[0]
        wanted = wanted.astype(jnp.int32)
        ids = jnp.arange(own_tiles, dtype=jnp.int32)
        before = jnp.sum(jnp.where(ids[None, :] < ids[:, None], wanted[None, :], 0), axis=1)
        return wanted, before

    ids = jnp.arange(own_tiles, dtype=jnp.int32)
    partner = me + 1 - 2 * row_place
    wanted, before = places(partner, row_place)
    picks = jnp.sum(
        jnp.where((wanted[None, :] > 0) & (before[None, :] == ids[:, None]), ids[None, :], 0), axis=1
    )
    _, arrival = places(me, 1 - row_place)
    within = listed % own_tiles
    is_local = listed // own_tiles == row_place
    place = jnp.sum(jnp.where(within[:, None] == ids[None, :], arrival[None, :], 0), axis=1)
    key = jnp.where(live, jnp.where(is_local, -1, place), 2 * own_tiles)
    ahead = (key[None, :] < key[:, None]) | (
        (key[None, :] == key[:, None]) & (slot_ids[None, :] < slot_ids[:, None])
    )
    rank = jnp.sum(ahead.astype(jnp.int32), axis=1)
    chosen = rank[None, :] == slot_ids[:, None]
    ordered = lambda v: jnp.sum(jnp.where(chosen, v[None, :], 0), axis=1)
    keys = ordered(key)
    rows = ordered(surv_rows[0, 0])
    cols = ordered(jnp.where(is_local, within, place))
    slots = ordered(slot_ids)

    half = TILE // 2
    keep = jnp.zeros((capacity + 1, half, TILE), jnp.float32)
    send = jnp.zeros((capacity + 1, half, TILE), jnp.float32)
    totals = sorted({max(4, own_tiles * n // 28) for n in TOTALS} | {own_tiles})
    branch = jnp.sum((largest > jnp.array(totals[:-1], jnp.int32)).astype(jnp.int32))
    operands = (x_act, grad_out, picks, keys, rows, cols, slots, keep, send)
    keep, send = lax.switch(
        branch, [functools.partial(exchange_and_square, total) for total in totals], operands
    )
    other = lax.ppermute(send, "tok", [(0, 1), (1, 0)])
    return (keep + other)[:capacity][None, None]


TOTALS = (8, 12, 14, 15, 16, 17, 18, 19, 20, 21, 22, 23, 24, 26, 28)


def solution(mesh):
    return functools.partial(choose, mesh)


def choose(mesh, x_act, grad_out, surv_rows, surv_cols, counts):
    own_columns = grad_out.shape[2] // (mesh.shape["tiles"] * mesh.shape["rows"])
    paired = (
        mesh.shape["rows"] == 2
        and mesh.shape["tok"] == 2
        and own_columns % TILE == 0
        and own_columns // TILE >= 4
    )
    return spread(mesh, on_pair if paired else on_device)(
        x_act, grad_out, surv_rows, surv_cols, counts
    )


def spread(mesh, body):
    return jax.shard_map(
        body,
        mesh=mesh,
        in_specs=(
            P("tok", "groups", "rows"),
            P("tok", "groups", ("tiles", "rows")),
            P(("groups", "tiles"), "rows", None),
            P(("groups", "tiles"), "rows", None),
            P(("groups", "tiles"), "rows"),
        ),
        out_specs=P(("groups", "tiles"), "rows", None, "tok", None),
        check_vma=False,
    )
```

```python
import functools

import jax
import jax.numpy as jnp
from jax import lax
from jax.experimental import pallas as pl
from jax.experimental.pallas import tpu as pltpu
from jax.sharding import PartitionSpec as P

TILE = 128


def square_tiles(x_tiles, panel_fetch, row_index, live_count, places, slot_total):
    tile_extent = x_tiles.shape[2]
    block_size = min(16, slot_total)
    result = jnp.zeros((slot_total, tile_extent, tile_extent), jnp.float32)

    def one_block(block_index, totals):
        first_slot = block_index * block_size
        rows_here = lax.dynamic_slice_in_dim(row_index, first_slot, block_size)
        x_panels = jnp.take(x_tiles, rows_here, axis=1)
        y_panels = panel_fetch(first_slot, block_size)
        gradients = jnp.einsum(
            "tnk,tnj->nkj", x_panels, y_panels, preferred_element_type=jnp.float32
        )
        is_live = first_slot + jnp.arange(block_size, dtype=jnp.int32) < live_count
        squares = jnp.where(is_live[:, None, None], gradients * gradients, 0.0)
        where_to = lax.dynamic_slice_in_dim(places, first_slot, block_size)
        return totals.at[where_to].set(squares)

    trip_count = (live_count + block_size - 1) // block_size
    return lax.fori_loop(0, trip_count, one_block, result)


def sum_samples(partial_value):
    return lax.psum_scatter(partial_value, "tok", scatter_dimension=1, tiled=True)


def on_device(x_act, grad_out, surv_rows, surv_cols, counts):
    tile_extent = TILE
    gathered = lax.all_gather(grad_out, "rows", axis=2, tiled=True)
    length_value = x_act.shape[1]
    x_tiles = x_act[0].reshape(length_value, -1, tile_extent)
    y_tiles = gathered[0].reshape(length_value, -1, tile_extent)
    row_listing = surv_rows[0, 0]
    cols_list = surv_cols[0, 0]
    live_here = counts[0, 0]
    capacity = row_listing.shape[0]
    keep_count = capacity // 2

    def from_own(first_slot, block_size):
        cols_here = lax.dynamic_slice_in_dim(cols_list, first_slot, block_size)
        return jnp.take(y_tiles, cols_here, axis=1)

    owners = lax.axis_size("tiles")
    position = lax.axis_index("tiles")
    deal_size = (capacity - keep_count) // owners
    own_places = jnp.arange(keep_count, dtype=jnp.int32)
    own_part = square_tiles(
        x_tiles,
        from_own,
        row_listing[:keep_count],
        jnp.minimum(live_here, keep_count),
        own_places,
        keep_count,
    )
    outbound_tiles = jnp.take(y_tiles, cols_list[keep_count:], axis=1)
    outbound_tiles = outbound_tiles.reshape(length_value, owners, deal_size, tile_extent)
    outbound_tiles = jnp.roll(outbound_tiles, position, axis=1).reshape(
        length_value, owners * deal_size, tile_extent
    )
    incoming = lax.all_to_all(outbound_tiles, "tiles", split_axis=1, concat_axis=1, tiled=True)
    all_rows, all_counts = (
        lax.all_gather(surv_rows, "tiles", axis=0, tiled=True),
        lax.all_gather(counts, "tiles", axis=0, tiled=True),
    )
    sources = jnp.arange(owners, dtype=jnp.int32)
    block_of = (position - sources) % owners
    slot_ids = (
        keep_count + block_of[:, None] * deal_size + jnp.arange(deal_size, dtype=jnp.int32)[None, :]
    )
    wanted_rows = jnp.take_along_axis(all_rows[:, 0, :], slot_ids, axis=1).reshape(-1)
    is_wanted = (slot_ids < all_counts[:, 0][:, None]).reshape(-1)
    ordering = jnp.argsort(1 - is_wanted.astype(jnp.int32), stable=True)
    wanted_total = jnp.sum(is_wanted.astype(jnp.int32))

    def from_incoming(first_slot, block_size):
        picks = lax.dynamic_slice_in_dim(ordering, first_slot, block_size)
        return jnp.take(incoming, picks, axis=1)

    helped = square_tiles(
        x_tiles, from_incoming, wanted_rows[ordering], wanted_total, ordering, owners * deal_size
    )
    returned_tiles = lax.all_to_all(helped, "tiles", split_axis=0, concat_axis=0, tiled=True)
    returned_tiles = returned_tiles.reshape(owners, deal_size, tile_extent, tile_extent)
    returned_tiles = jnp.roll(returned_tiles, -position, axis=0).reshape(
        owners * deal_size, tile_extent, tile_extent
    )
    fisher = sum_samples(jnp.concatenate([own_part, returned_tiles], axis=0))
    return fisher[None, None]


def share_body(listed_ref, all_ref, send_sems, recv_sems, own_sem):
    tiles, row_count = lax.axis_size("tiles"), lax.axis_size("rows")
    owners = all_ref.shape[0]
    me = (
        lax.axis_index("groups") * tiles + lax.axis_index("tiles")
    ) * row_count + lax.axis_index("rows")

    def peer(step):
        there = lax.rem(me + step, owners)
        return {
            "groups": there // (tiles * row_count),
            "tiles": lax.rem(there // row_count, tiles),
            "rows": lax.rem(there, row_count),
        }

    barrier = pltpu.get_barrier_semaphore()
    for step in range(1, owners):
        pl.semaphore_signal(
            barrier, inc=1, device_id=peer(step), device_id_type=pl.DeviceIdType.MESH
        )
    pl.semaphore_wait(barrier, owners - 1)
    own = pltpu.make_async_copy(listed_ref, all_ref.at[me], own_sem)
    own.start()
    copies = []
    for step in range(1, owners):
        copy = pltpu.make_async_remote_copy(
            src_ref=listed_ref,
            dst_ref=all_ref.at[me],
            send_sem=send_sems.at[step],
            recv_sem=recv_sems.at[step],
            device_id=peer(step),
            device_id_type=pl.DeviceIdType.MESH,
        )
        copy.start()
        copies.append(copy)
    own.wait()
    for copy in copies:
        copy.wait()


def share_lists(listed):
    owners = lax.axis_size("groups") * lax.axis_size("tiles") * lax.axis_size("rows")
    capacity = listed.shape[0]
    lanes = -(-capacity // 128) * 128
    row = jnp.broadcast_to(jnp.pad(listed, (0, lanes - capacity))[None, :], (8, lanes))
    shared = pl.pallas_call(
        share_body,
        out_shape=jax.ShapeDtypeStruct((owners, 8, lanes), jnp.int32),
        in_specs=[pl.BlockSpec(memory_space=pltpu.VMEM)],
        out_specs=pl.BlockSpec(memory_space=pltpu.VMEM),
        scratch_shapes=[
            pltpu.SemaphoreType.DMA((owners,)),
            pltpu.SemaphoreType.DMA((owners,)),
            pltpu.SemaphoreType.DMA,
        ],
        compiler_params=pltpu.CompilerParams(collective_id=3, has_side_effects=True),
        name="share_lists",
    )(row)
    return shared[:, 0, :capacity]


def pack_body(pick_ref, y_ref, out_ref, held, in_sems, out_sems):
    chosen = out_ref.shape[0]
    loads = []
    for i in range(chosen):
        first = pl.multiple_of(pick_ref[i] * TILE, TILE)
        load = pltpu.make_async_copy(y_ref.at[0, :, pl.ds(first, TILE)], held.at[i], in_sems.at[i])
        load.start()
        loads.append(load)
    stores = []
    for i in range(chosen):
        loads[i].wait()
        store = pltpu.make_async_copy(held.at[i], out_ref.at[i], out_sems.at[i])
        store.start()
        stores.append(store)
    for store in stores:
        store.wait()


def pack_panels(y, picks):
    tokens = y.shape[1]
    chosen = picks.shape[0]
    return pl.pallas_call(
        pack_body,
        out_shape=jax.ShapeDtypeStruct((chosen, tokens, TILE), y.dtype),
        in_specs=[pl.BlockSpec(memory_space=pltpu.SMEM), pl.BlockSpec(memory_space=pl.ANY)],
        out_specs=pl.BlockSpec(memory_space=pl.ANY),
        scratch_shapes=[
            pltpu.VMEM((chosen, tokens, TILE), y.dtype),
            pltpu.SemaphoreType.DMA((chosen,)),
            pltpu.SemaphoreType.DMA((chosen,)),
        ],
        cost_estimate=pl.CostEstimate(
            flops=0, bytes_accessed=4 * chosen * tokens * TILE, transcendentals=0
        ),
        name="pack_panels",
    )(picks, y)


def square_body(apart, steps_ref, rows_ref, cols_ref, slots_ref, x_ref, y_ref, a_ref, b_ref, keep_ref, send_ref):
    del a_ref, b_ref
    tokens = x_ref.shape[1]
    half = TILE // 2
    first = lax.axis_index("tok") == 0

    def one_slot(x_tile, y_tile, keep_tile, send_tile):
        gradient = lax.dot_general(
            x_tile[0], y_tile[0], (((0,), (0,)), ((), ())), preferred_element_type=jnp.float32
        )
        squares = gradient * gradient

        @pl.when(first)
        def _():
            keep_tile[0] = squares[:half]
            send_tile[0] = squares[half:]

        @pl.when(jnp.logical_not(first))
        def _():
            keep_tile[0] = squares[half:]
            send_tile[0] = squares[:half]

    y_map = (lambda i: (cols_ref[i], 0, 0)) if apart else (lambda i: (0, 0, cols_ref[i]))
    out_spec = pl.BlockSpec((1, half, TILE), lambda i: (slots_ref[i], 0, 0))
    pltpu.emit_pipeline(
        one_slot,
        grid=(steps_ref[0],),
        in_specs=[
            pl.BlockSpec((1, tokens, TILE), lambda i: (0, 0, rows_ref[i])),
            pl.BlockSpec((1, tokens, TILE), y_map),
        ],
        out_specs=[out_spec, out_spec],
    )(x_ref, y_ref, keep_ref, send_ref)


def square_slots(x, y, steps, rows, cols, slots, keep, send, panels_apart):
    tokens = x.shape[1]
    any_spec = pl.BlockSpec(memory_space=pl.ANY)
    smem_spec = pl.BlockSpec(memory_space=pltpu.SMEM)
    expected = max(1, rows.shape[0] // (8 if panels_apart else 2))
    return pl.pallas_call(
        functools.partial(square_body, panels_apart),
        out_shape=(
            jax.ShapeDtypeStruct(keep.shape, keep.dtype),
            jax.ShapeDtypeStruct(send.shape, send.dtype),
        ),
        in_specs=[smem_spec] * 4 + [any_spec] * 4,
        out_specs=(any_spec, any_spec),
        input_output_aliases={6: 0, 7: 1},
        cost_estimate=pl.CostEstimate(
            flops=expected * 2 * tokens * TILE * TILE,
            bytes_accessed=expected * (4 * tokens * TILE + 4 * TILE * TILE),
            transcendentals=0,
        ),
        name="square_slots",
    )(steps.reshape(1), rows, cols, slots, x, y, keep, send)


def chunk_sizes(total):
    last = max(1, total // 8)
    rest = total - last
    parts = 3
    sizes = [rest // parts + (1 if i < rest % parts else 0) for i in range(parts)]
    return sizes + [last]


def exchange_and_square(total, operands):
    x, y, picks, keys, rows, cols, slots, keep, send = operands
    sizes = chunk_sizes(total)
    swap = [(0, 1), (1, 0)]
    arrived = []
    first = 0
    for size in sizes:
        packed = pack_panels(y, picks[first : first + size])
        arrived.append(lax.ppermute(packed, "rows", swap))
        first += size
    capacity = rows.shape[0]
    dummy = keep.shape[0] - 1

    def phase(panels, low, high, keep, send, apart):
        begin = jnp.sum((keys < low).astype(jnp.int32))
        steps = jnp.sum((keys < high).astype(jnp.int32)) - begin
        live = steps > 0
        roll = lambda v: lax.dynamic_slice(jnp.concatenate([v, v]), (begin,), (capacity,))
        here_cols = roll(cols) - (low if apart else 0)
        here_cols = jnp.where(live, here_cols, 0)
        here_cols = jnp.clip(here_cols, 0, (high - low - 1) if apart else y.shape[2] // TILE - 1)
        here_slots = jnp.where(live, roll(slots), dummy)
        return square_slots(
            x, panels, jnp.maximum(steps, 1), roll(rows), here_cols, here_slots, keep, send, apart
        )

    keep, send = phase(y, -1, 0, keep, send, False)
    first = 0
    for size, panels in zip(sizes, arrived):
        keep, send = phase(panels, first, first + size, keep, send, True)
        first += size
    return keep, send


def on_pair(x_act, grad_out, surv_rows, surv_cols, counts):
    own_tiles = grad_out.shape[2] // TILE
    capacity = surv_rows.shape[2]
    row_place = lax.axis_index("rows")
    slot_ids = jnp.arange(capacity, dtype=jnp.int32)
    live = slot_ids < counts[0, 0]
    listed = jnp.where(live, surv_cols[0, 0], -1)
    everyone = share_lists(listed)
    columns = jnp.arange(2 * own_tiles, dtype=jnp.int32)
    needed = jnp.any(everyone[:, None, :] == columns[None, :, None], axis=2)
    owner_rows = (jnp.arange(everyone.shape[0], dtype=jnp.int32) % 2)[:, None]
    remote = needed & ((columns // own_tiles)[None, :] != owner_rows)
    largest = jnp.max(jnp.sum(remote.astype(jnp.int32), axis=1))

    me = (lax.axis_index("groups") * lax.axis_size("tiles") + lax.axis_index("tiles")) * 2 + row_place

    def places(owner, holder):
        wanted = lax.dynamic_slice(remote, (owner, holder * own_tiles), (1, own_tiles))[0]
        wanted = wanted.astype(jnp.int32)
        ids = jnp.arange(own_tiles, dtype=jnp.int32)
        before = jnp.sum(jnp.where(ids[None, :] < ids[:, None], wanted[None, :], 0), axis=1)
        return wanted, before

    ids = jnp.arange(own_tiles, dtype=jnp.int32)
    partner = me + 1 - 2 * row_place
    wanted, before = places(partner, row_place)
    picks = jnp.sum(
        jnp.where((wanted[None, :] > 0) & (before[None, :] == ids[:, None]), ids[None, :], 0), axis=1
    )
    _, arrival = places(me, 1 - row_place)
    within = listed % own_tiles
    is_local = listed // own_tiles == row_place
    place = jnp.sum(jnp.where(within[:, None] == ids[None, :], arrival[None, :], 0), axis=1)
    key = jnp.where(live, jnp.where(is_local, -1, place), 2 * own_tiles)
    ahead = (key[None, :] < key[:, None]) | (
        (key[None, :] == key[:, None]) & (slot_ids[None, :] < slot_ids[:, None])
    )
    rank = jnp.sum(ahead.astype(jnp.int32), axis=1)
    chosen = rank[None, :] == slot_ids[:, None]
    ordered = lambda v: jnp.sum(jnp.where(chosen, v[None, :], 0), axis=1)
    keys = ordered(key)
    rows = ordered(surv_rows[0, 0])
    cols = ordered(jnp.where(is_local, within, place))
    slots = ordered(slot_ids)

    half = TILE // 2
    keep = jnp.zeros((capacity + 1, half, TILE), jnp.float32)
    send = jnp.zeros((capacity + 1, half, TILE), jnp.float32)
    totals = sorted({max(4, own_tiles * n // 28) for n in TOTALS} | {own_tiles})
    branch = jnp.sum((largest > jnp.array(totals[:-1], jnp.int32)).astype(jnp.int32))
    operands = (x_act, grad_out, picks, keys, rows, cols, slots, keep, send)
    keep, send = lax.switch(
        branch, [functools.partial(exchange_and_square, total) for total in totals], operands
    )
    other = lax.ppermute(send, "tok", [(0, 1), (1, 0)])
    return (keep + other)[:capacity][None, None]


TOTALS = (8, 12, 14, 15, 16, 17, 18, 19, 20, 21, 22, 23, 24, 26, 28)


def solution(mesh):
    return functools.partial(choose, mesh)


def choose(mesh, x_act, grad_out, surv_rows, surv_cols, counts):
    own_columns = grad_out.shape[2] // (mesh.shape["tiles"] * mesh.shape["rows"])
    paired = (
        mesh.shape["rows"] == 2
        and mesh.shape["tok"] == 2
        and own_columns % TILE == 0
        and own_columns // TILE >= 4
    )
    return spread(mesh, on_pair if paired else on_device)(
        x_act, grad_out, surv_rows, surv_cols, counts
    )


def spread(mesh, body):
    return jax.shard_map(
        body,
        mesh=mesh,
        in_specs=(
            P("tok", "groups", "rows"),
            P("tok", "groups", ("tiles", "rows")),
            P(("groups", "tiles"), "rows", None),
            P(("groups", "tiles"), "rows", None),
            P(("groups", "tiles"), "rows"),
        ),
        out_specs=P(("groups", "tiles"), "rows", None, "tok", None),
        check_vma=False,
    )
```

```python
import functools

import jax
import jax.numpy as jnp
from jax import lax
from jax.experimental import pallas as pl
from jax.experimental.pallas import tpu as pltpu
from jax.sharding import PartitionSpec as P

TILE = 128


def square_tiles(x_tiles, panel_fetch, row_index, live_count, places, slot_total):
    tile_extent = x_tiles.shape[2]
    block_size = min(16, slot_total)
    result = jnp.zeros((slot_total, tile_extent, tile_extent), jnp.float32)

    def one_block(block_index, totals):
        first_slot = block_index * block_size
        rows_here = lax.dynamic_slice_in_dim(row_index, first_slot, block_size)
        x_panels = jnp.take(x_tiles, rows_here, axis=1)
        y_panels = panel_fetch(first_slot, block_size)
        gradients = jnp.einsum(
            "tnk,tnj->nkj", x_panels, y_panels, preferred_element_type=jnp.float32
        )
        is_live = first_slot + jnp.arange(block_size, dtype=jnp.int32) < live_count
        squares = jnp.where(is_live[:, None, None], gradients * gradients, 0.0)
        where_to = lax.dynamic_slice_in_dim(places, first_slot, block_size)
        return totals.at[where_to].set(squares)

    trip_count = (live_count + block_size - 1) // block_size
    return lax.fori_loop(0, trip_count, one_block, result)


def sum_samples(partial_value):
    return lax.psum_scatter(partial_value, "tok", scatter_dimension=1, tiled=True)


def on_device(x_act, grad_out, surv_rows, surv_cols, counts):
    tile_extent = TILE
    gathered = lax.all_gather(grad_out, "rows", axis=2, tiled=True)
    length_value = x_act.shape[1]
    x_tiles = x_act[0].reshape(length_value, -1, tile_extent)
    y_tiles = gathered[0].reshape(length_value, -1, tile_extent)
    row_listing = surv_rows[0, 0]
    cols_list = surv_cols[0, 0]
    live_here = counts[0, 0]
    capacity = row_listing.shape[0]
    keep_count = capacity // 2

    def from_own(first_slot, block_size):
        cols_here = lax.dynamic_slice_in_dim(cols_list, first_slot, block_size)
        return jnp.take(y_tiles, cols_here, axis=1)

    owners = lax.axis_size("tiles")
    position = lax.axis_index("tiles")
    deal_size = (capacity - keep_count) // owners
    own_places = jnp.arange(keep_count, dtype=jnp.int32)
    own_part = square_tiles(
        x_tiles,
        from_own,
        row_listing[:keep_count],
        jnp.minimum(live_here, keep_count),
        own_places,
        keep_count,
    )
    outbound_tiles = jnp.take(y_tiles, cols_list[keep_count:], axis=1)
    outbound_tiles = outbound_tiles.reshape(length_value, owners, deal_size, tile_extent)
    outbound_tiles = jnp.roll(outbound_tiles, position, axis=1).reshape(
        length_value, owners * deal_size, tile_extent
    )
    incoming = lax.all_to_all(outbound_tiles, "tiles", split_axis=1, concat_axis=1, tiled=True)
    all_rows, all_counts = (
        lax.all_gather(surv_rows, "tiles", axis=0, tiled=True),
        lax.all_gather(counts, "tiles", axis=0, tiled=True),
    )
    sources = jnp.arange(owners, dtype=jnp.int32)
    block_of = (position - sources) % owners
    slot_ids = (
        keep_count + block_of[:, None] * deal_size + jnp.arange(deal_size, dtype=jnp.int32)[None, :]
    )
    wanted_rows = jnp.take_along_axis(all_rows[:, 0, :], slot_ids, axis=1).reshape(-1)
    is_wanted = (slot_ids < all_counts[:, 0][:, None]).reshape(-1)
    ordering = jnp.argsort(1 - is_wanted.astype(jnp.int32), stable=True)
    wanted_total = jnp.sum(is_wanted.astype(jnp.int32))

    def from_incoming(first_slot, block_size):
        picks = lax.dynamic_slice_in_dim(ordering, first_slot, block_size)
        return jnp.take(incoming, picks, axis=1)

    helped = square_tiles(
        x_tiles, from_incoming, wanted_rows[ordering], wanted_total, ordering, owners * deal_size
    )
    returned_tiles = lax.all_to_all(helped, "tiles", split_axis=0, concat_axis=0, tiled=True)
    returned_tiles = returned_tiles.reshape(owners, deal_size, tile_extent, tile_extent)
    returned_tiles = jnp.roll(returned_tiles, -position, axis=0).reshape(
        owners * deal_size, tile_extent, tile_extent
    )
    fisher = sum_samples(jnp.concatenate([own_part, returned_tiles], axis=0))
    return fisher[None, None]


def share_body(listed_ref, all_ref, send_sems, recv_sems, own_sem):
    tiles, row_count = lax.axis_size("tiles"), lax.axis_size("rows")
    owners = all_ref.shape[0]
    me = (
        lax.axis_index("groups") * tiles + lax.axis_index("tiles")
    ) * row_count + lax.axis_index("rows")

    def peer(step):
        there = lax.rem(me + step, owners)
        return {
            "groups": there // (tiles * row_count),
            "tiles": lax.rem(there // row_count, tiles),
            "rows": lax.rem(there, row_count),
        }

    barrier = pltpu.get_barrier_semaphore()
    for step in range(1, owners):
        pl.semaphore_signal(
            barrier, inc=1, device_id=peer(step), device_id_type=pl.DeviceIdType.MESH
        )
    pl.semaphore_wait(barrier, owners - 1)
    own = pltpu.make_async_copy(listed_ref, all_ref.at[me], own_sem)
    own.start()
    copies = []
    for step in range(1, owners):
        copy = pltpu.make_async_remote_copy(
            src_ref=listed_ref,
            dst_ref=all_ref.at[me],
            send_sem=send_sems.at[step],
            recv_sem=recv_sems.at[step],
            device_id=peer(step),
            device_id_type=pl.DeviceIdType.MESH,
        )
        copy.start()
        copies.append(copy)
    own.wait()
    for copy in copies:
        copy.wait()


def share_lists(listed):
    owners = lax.axis_size("groups") * lax.axis_size("tiles") * lax.axis_size("rows")
    capacity = listed.shape[0]
    lanes = -(-capacity // 128) * 128
    row = jnp.broadcast_to(jnp.pad(listed, (0, lanes - capacity))[None, :], (8, lanes))
    shared = pl.pallas_call(
        share_body,
        out_shape=jax.ShapeDtypeStruct((owners, 8, lanes), jnp.int32),
        in_specs=[pl.BlockSpec(memory_space=pltpu.VMEM)],
        out_specs=pl.BlockSpec(memory_space=pltpu.VMEM),
        scratch_shapes=[
            pltpu.SemaphoreType.DMA((owners,)),
            pltpu.SemaphoreType.DMA((owners,)),
            pltpu.SemaphoreType.DMA,
        ],
        compiler_params=pltpu.CompilerParams(collective_id=3, has_side_effects=True),
        name="share_lists",
    )(row)
    return shared[:, 0, :capacity]


def pack_body(pick_ref, y_ref, out_ref, held, in_sems, out_sems):
    chosen = out_ref.shape[0]
    loads = []
    for i in range(chosen):
        first = pl.multiple_of(pick_ref[i] * TILE, TILE)
        load = pltpu.make_async_copy(y_ref.at[0, :, pl.ds(first, TILE)], held.at[i], in_sems.at[i])
        load.start()
        loads.append(load)
    stores = []
    for i in range(chosen):
        loads[i].wait()
        store = pltpu.make_async_copy(held.at[i], out_ref.at[i], out_sems.at[i])
        store.start()
        stores.append(store)
    for store in stores:
        store.wait()


def pack_panels(y, picks):
    tokens = y.shape[1]
    chosen = picks.shape[0]
    return pl.pallas_call(
        pack_body,
        out_shape=jax.ShapeDtypeStruct((chosen, tokens, TILE), y.dtype),
        in_specs=[pl.BlockSpec(memory_space=pltpu.SMEM), pl.BlockSpec(memory_space=pl.ANY)],
        out_specs=pl.BlockSpec(memory_space=pl.ANY),
        scratch_shapes=[
            pltpu.VMEM((chosen, tokens, TILE), y.dtype),
            pltpu.SemaphoreType.DMA((chosen,)),
            pltpu.SemaphoreType.DMA((chosen,)),
        ],
        cost_estimate=pl.CostEstimate(
            flops=0, bytes_accessed=4 * chosen * tokens * TILE, transcendentals=0
        ),
        name="pack_panels",
    )(picks, y)


def square_body(apart, steps_ref, rows_ref, cols_ref, slots_ref, x_ref, y_ref, a_ref, b_ref, keep_ref, send_ref):
    del a_ref, b_ref
    tokens = x_ref.shape[1]
    half = TILE // 2
    first = lax.axis_index("tok") == 0

    def one_slot(x_tile, y_tile, keep_tile, send_tile):
        gradient = lax.dot_general(
            x_tile[0], y_tile[0], (((0,), (0,)), ((), ())), preferred_element_type=jnp.float32
        )
        squares = gradient * gradient

        @pl.when(first)
        def _():
            keep_tile[0] = squares[:half]
            send_tile[0] = squares[half:]

        @pl.when(jnp.logical_not(first))
        def _():
            keep_tile[0] = squares[half:]
            send_tile[0] = squares[:half]

    y_map = (lambda i: (cols_ref[i], 0, 0)) if apart else (lambda i: (0, 0, cols_ref[i]))
    out_spec = pl.BlockSpec((1, half, TILE), lambda i: (slots_ref[i], 0, 0))
    pltpu.emit_pipeline(
        one_slot,
        grid=(steps_ref[0],),
        in_specs=[
            pl.BlockSpec((1, tokens, TILE), lambda i: (0, 0, rows_ref[i])),
            pl.BlockSpec((1, tokens, TILE), y_map),
        ],
        out_specs=[out_spec, out_spec],
    )(x_ref, y_ref, keep_ref, send_ref)


def square_slots(x, y, steps, rows, cols, slots, keep, send, panels_apart):
    tokens = x.shape[1]
    any_spec = pl.BlockSpec(memory_space=pl.ANY)
    smem_spec = pl.BlockSpec(memory_space=pltpu.SMEM)
    expected = max(1, rows.shape[0] // (8 if panels_apart else 2))
    return pl.pallas_call(
        functools.partial(square_body, panels_apart),
        out_shape=(
            jax.ShapeDtypeStruct(keep.shape, keep.dtype),
            jax.ShapeDtypeStruct(send.shape, send.dtype),
        ),
        in_specs=[smem_spec] * 4 + [any_spec] * 4,
        out_specs=(any_spec, any_spec),
        input_output_aliases={6: 0, 7: 1},
        cost_estimate=pl.CostEstimate(
            flops=expected * 2 * tokens * TILE * TILE,
            bytes_accessed=expected * (4 * tokens * TILE + 4 * TILE * TILE),
            transcendentals=0,
        ),
        name="square_slots",
    )(steps.reshape(1), rows, cols, slots, x, y, keep, send)


def chunk_sizes(total):
    last = max(1, total // 8)
    rest = total - last
    parts = 3
    sizes = [rest // parts + (1 if i < rest % parts else 0) for i in range(parts)]
    return sizes + [last]


def exchange_and_square(total, operands):
    x, y, early, picks, keys, rows, cols, slots, keep, send = operands
    sizes = chunk_sizes(total)
    swap = [(0, 1), (1, 0)]
    arrived = []
    first = 0
    for size in sizes:
        packed = pack_panels(y, picks[first : first + size])
        arrived.append(lax.ppermute(packed, "rows", swap))
        first += size
    capacity = rows.shape[0]
    dummy = keep.shape[0] - 1

    def phase(panels, low, high, keep, send, apart):
        begin = jnp.sum((keys < low).astype(jnp.int32))
        steps = jnp.sum((keys < high).astype(jnp.int32)) - begin
        live = steps > 0
        roll = lambda v: lax.dynamic_slice(jnp.concatenate([v, v]), (begin,), (capacity,))
        here_cols = roll(cols) - (low if apart else 0)
        here_cols = jnp.where(live, here_cols, 0)
        here_cols = jnp.clip(here_cols, 0, (high - low - 1) if apart else panels.shape[2] // TILE - 1)
        here_slots = jnp.where(live, roll(slots), dummy)
        return square_slots(
            x, panels, jnp.maximum(steps, 1), roll(rows), here_cols, here_slots, keep, send, apart
        )

    keep, send = phase(y, -2, -1, keep, send, False)
    keep, send = phase(early, -1, 0, keep, send, False)
    first = 0
    for size, panels in zip(sizes, arrived):
        keep, send = phase(panels, first, first + size, keep, send, True)
        first += size
    return keep, send


def on_pair(x_act, grad_out, surv_rows, surv_cols, counts):
    own_tiles = grad_out.shape[2] // TILE
    early = lax.ppermute(grad_out[:, :, : HEAD * TILE], "rows", [(0, 1), (1, 0)])
    capacity = surv_rows.shape[2]
    row_place = lax.axis_index("rows")
    slot_ids = jnp.arange(capacity, dtype=jnp.int32)
    live = slot_ids < counts[0, 0]
    listed = jnp.where(live, surv_cols[0, 0], -1)
    everyone = share_lists(listed)
    columns = jnp.arange(2 * own_tiles, dtype=jnp.int32)
    needed = jnp.any(everyone[:, None, :] == columns[None, :, None], axis=2)
    owner_rows = (jnp.arange(everyone.shape[0], dtype=jnp.int32) % 2)[:, None]
    remote = needed & ((columns // own_tiles)[None, :] != owner_rows)
    remote = remote & (columns % own_tiles >= HEAD)[None, :]
    largest = jnp.max(jnp.sum(remote.astype(jnp.int32), axis=1))

    me = (lax.axis_index("groups") * lax.axis_size("tiles") + lax.axis_index("tiles")) * 2 + row_place

    def places(owner, holder):
        wanted = lax.dynamic_slice(remote, (owner, holder * own_tiles), (1, own_tiles))[0]
        wanted = wanted.astype(jnp.int32)
        ids = jnp.arange(own_tiles, dtype=jnp.int32)
        before = jnp.sum(jnp.where(ids[None, :] < ids[:, None], wanted[None, :], 0), axis=1)
        return wanted, before

    ids = jnp.arange(own_tiles, dtype=jnp.int32)
    partner = me + 1 - 2 * row_place
    wanted, before = places(partner, row_place)
    picks = jnp.sum(
        jnp.where((wanted[None, :] > 0) & (before[None, :] == ids[:, None]), ids[None, :], 0), axis=1
    )
    _, arrival = places(me, 1 - row_place)
    within = listed % own_tiles
    is_local = listed // own_tiles == row_place
    place = jnp.sum(jnp.where(within[:, None] == ids[None, :], arrival[None, :], 0), axis=1)
    is_early = ~is_local & (within < HEAD)
    key = jnp.where(is_local, -2, jnp.where(is_early, -1, place))
    key = jnp.where(live, key, 2 * own_tiles)
    ahead = (key[None, :] < key[:, None]) | (
        (key[None, :] == key[:, None]) & (slot_ids[None, :] < slot_ids[:, None])
    )
    rank = jnp.sum(ahead.astype(jnp.int32), axis=1)
    chosen = rank[None, :] == slot_ids[:, None]
    ordered = lambda v: jnp.sum(jnp.where(chosen, v[None, :], 0), axis=1)
    keys = ordered(key)
    rows = ordered(surv_rows[0, 0])
    cols = ordered(jnp.where(is_local | is_early, within, place))
    slots = ordered(slot_ids)

    half = TILE // 2
    keep = jnp.zeros((capacity + 1, half, TILE), jnp.float32)
    send = jnp.zeros((capacity + 1, half, TILE), jnp.float32)
    totals = sorted({max(4, own_tiles * n // 28) for n in TOTALS} | {own_tiles})
    branch = jnp.sum((largest > jnp.array(totals[:-1], jnp.int32)).astype(jnp.int32))
    operands = (x_act, grad_out, early, picks, keys, rows, cols, slots, keep, send)
    keep, send = lax.switch(
        branch, [functools.partial(exchange_and_square, total) for total in totals], operands
    )
    other = lax.ppermute(send, "tok", [(0, 1), (1, 0)])
    return (keep + other)[:capacity][None, None]


HEAD = 4
TOTALS = (8, 10, 12, 13, 14, 15, 16, 17, 18, 19, 20, 22)


def solution(mesh):
    return functools.partial(choose, mesh)


def choose(mesh, x_act, grad_out, surv_rows, surv_cols, counts):
    own_columns = grad_out.shape[2] // (mesh.shape["tiles"] * mesh.shape["rows"])
    paired = (
        mesh.shape["rows"] == 2
        and mesh.shape["tok"] == 2
        and own_columns % TILE == 0
        and own_columns // TILE >= 4
    )
    return spread(mesh, on_pair if paired else on_device)(
        x_act, grad_out, surv_rows, surv_cols, counts
    )


def spread(mesh, body):
    return jax.shard_map(
        body,
        mesh=mesh,
        in_specs=(
            P("tok", "groups", "rows"),
            P("tok", "groups", ("tiles", "rows")),
            P(("groups", "tiles"), "rows", None),
            P(("groups", "tiles"), "rows", None),
            P(("groups", "tiles"), "rows"),
        ),
        out_specs=P(("groups", "tiles"), "rows", None, "tok", None),
        check_vma=False,
    )
```

```python
import functools

import jax
import jax.numpy as jnp
from jax import lax
from jax.experimental import pallas as pl
from jax.experimental.pallas import tpu as pltpu
from jax.sharding import PartitionSpec as P

TILE = 128


def square_tiles(x_tiles, panel_fetch, row_index, live_count, places, slot_total):
    tile_extent = x_tiles.shape[2]
    block_size = min(16, slot_total)
    result = jnp.zeros((slot_total, tile_extent, tile_extent), jnp.float32)

    def one_block(block_index, totals):
        first_slot = block_index * block_size
        rows_here = lax.dynamic_slice_in_dim(row_index, first_slot, block_size)
        x_panels = jnp.take(x_tiles, rows_here, axis=1)
        y_panels = panel_fetch(first_slot, block_size)
        gradients = jnp.einsum(
            "tnk,tnj->nkj", x_panels, y_panels, preferred_element_type=jnp.float32
        )
        is_live = first_slot + jnp.arange(block_size, dtype=jnp.int32) < live_count
        squares = jnp.where(is_live[:, None, None], gradients * gradients, 0.0)
        where_to = lax.dynamic_slice_in_dim(places, first_slot, block_size)
        return totals.at[where_to].set(squares)

    trip_count = (live_count + block_size - 1) // block_size
    return lax.fori_loop(0, trip_count, one_block, result)


def sum_samples(partial_value):
    return lax.psum_scatter(partial_value, "tok", scatter_dimension=1, tiled=True)


def on_device(x_act, grad_out, surv_rows, surv_cols, counts):
    tile_extent = TILE
    gathered = lax.all_gather(grad_out, "rows", axis=2, tiled=True)
    length_value = x_act.shape[1]
    x_tiles = x_act[0].reshape(length_value, -1, tile_extent)
    y_tiles = gathered[0].reshape(length_value, -1, tile_extent)
    row_listing = surv_rows[0, 0]
    cols_list = surv_cols[0, 0]
    live_here = counts[0, 0]
    capacity = row_listing.shape[0]
    keep_count = capacity // 2

    def from_own(first_slot, block_size):
        cols_here = lax.dynamic_slice_in_dim(cols_list, first_slot, block_size)
        return jnp.take(y_tiles, cols_here, axis=1)

    owners = lax.axis_size("tiles")
    position = lax.axis_index("tiles")
    deal_size = (capacity - keep_count) // owners
    own_places = jnp.arange(keep_count, dtype=jnp.int32)
    own_part = square_tiles(
        x_tiles,
        from_own,
        row_listing[:keep_count],
        jnp.minimum(live_here, keep_count),
        own_places,
        keep_count,
    )
    outbound_tiles = jnp.take(y_tiles, cols_list[keep_count:], axis=1)
    outbound_tiles = outbound_tiles.reshape(length_value, owners, deal_size, tile_extent)
    outbound_tiles = jnp.roll(outbound_tiles, position, axis=1).reshape(
        length_value, owners * deal_size, tile_extent
    )
    incoming = lax.all_to_all(outbound_tiles, "tiles", split_axis=1, concat_axis=1, tiled=True)
    all_rows, all_counts = (
        lax.all_gather(surv_rows, "tiles", axis=0, tiled=True),
        lax.all_gather(counts, "tiles", axis=0, tiled=True),
    )
    sources = jnp.arange(owners, dtype=jnp.int32)
    block_of = (position - sources) % owners
    slot_ids = (
        keep_count + block_of[:, None] * deal_size + jnp.arange(deal_size, dtype=jnp.int32)[None, :]
    )
    wanted_rows = jnp.take_along_axis(all_rows[:, 0, :], slot_ids, axis=1).reshape(-1)
    is_wanted = (slot_ids < all_counts[:, 0][:, None]).reshape(-1)
    ordering = jnp.argsort(1 - is_wanted.astype(jnp.int32), stable=True)
    wanted_total = jnp.sum(is_wanted.astype(jnp.int32))

    def from_incoming(first_slot, block_size):
        picks = lax.dynamic_slice_in_dim(ordering, first_slot, block_size)
        return jnp.take(incoming, picks, axis=1)

    helped = square_tiles(
        x_tiles, from_incoming, wanted_rows[ordering], wanted_total, ordering, owners * deal_size
    )
    returned_tiles = lax.all_to_all(helped, "tiles", split_axis=0, concat_axis=0, tiled=True)
    returned_tiles = returned_tiles.reshape(owners, deal_size, tile_extent, tile_extent)
    returned_tiles = jnp.roll(returned_tiles, -position, axis=0).reshape(
        owners * deal_size, tile_extent, tile_extent
    )
    fisher = sum_samples(jnp.concatenate([own_part, returned_tiles], axis=0))
    return fisher[None, None]


def share_body(listed_ref, all_ref, send_sems, recv_sems, own_sem):
    tiles, row_count = lax.axis_size("tiles"), lax.axis_size("rows")
    owners = all_ref.shape[0]
    me = (
        lax.axis_index("groups") * tiles + lax.axis_index("tiles")
    ) * row_count + lax.axis_index("rows")

    def peer(step):
        there = lax.rem(me + step, owners)
        return {
            "groups": there // (tiles * row_count),
            "tiles": lax.rem(there // row_count, tiles),
            "rows": lax.rem(there, row_count),
        }

    barrier = pltpu.get_barrier_semaphore()
    for step in range(1, owners):
        pl.semaphore_signal(
            barrier, inc=1, device_id=peer(step), device_id_type=pl.DeviceIdType.MESH
        )
    pl.semaphore_wait(barrier, owners - 1)
    own = pltpu.make_async_copy(listed_ref, all_ref.at[me], own_sem)
    own.start()
    copies = []
    for step in range(1, owners):
        copy = pltpu.make_async_remote_copy(
            src_ref=listed_ref,
            dst_ref=all_ref.at[me],
            send_sem=send_sems.at[step],
            recv_sem=recv_sems.at[step],
            device_id=peer(step),
            device_id_type=pl.DeviceIdType.MESH,
        )
        copy.start()
        copies.append(copy)
    own.wait()
    for copy in copies:
        copy.wait()


def share_lists(listed):
    owners = lax.axis_size("groups") * lax.axis_size("tiles") * lax.axis_size("rows")
    capacity = listed.shape[0]
    lanes = -(-capacity // 128) * 128
    row = jnp.broadcast_to(jnp.pad(listed, (0, lanes - capacity))[None, :], (8, lanes))
    shared = pl.pallas_call(
        share_body,
        out_shape=jax.ShapeDtypeStruct((owners, 8, lanes), jnp.int32),
        in_specs=[pl.BlockSpec(memory_space=pltpu.VMEM)],
        out_specs=pl.BlockSpec(memory_space=pltpu.VMEM),
        scratch_shapes=[
            pltpu.SemaphoreType.DMA((owners,)),
            pltpu.SemaphoreType.DMA((owners,)),
            pltpu.SemaphoreType.DMA,
        ],
        compiler_params=pltpu.CompilerParams(collective_id=3, has_side_effects=True),
        name="share_lists",
    )(row)
    return shared[:, 0, :capacity]


def pack_body(pick_ref, y_ref, out_ref, held, in_sems, out_sems):
    chosen = out_ref.shape[0]
    loads = []
    for i in range(chosen):
        first = pl.multiple_of(pick_ref[i] * TILE, TILE)
        load = pltpu.make_async_copy(y_ref.at[0, :, pl.ds(first, TILE)], held.at[i], in_sems.at[i])
        load.start()
        loads.append(load)
    stores = []
    for i in range(chosen):
        loads[i].wait()
        store = pltpu.make_async_copy(held.at[i], out_ref.at[i], out_sems.at[i])
        store.start()
        stores.append(store)
    for store in stores:
        store.wait()


def pack_panels(y, picks):
    tokens = y.shape[1]
    chosen = picks.shape[0]
    return pl.pallas_call(
        pack_body,
        out_shape=jax.ShapeDtypeStruct((chosen, tokens, TILE), y.dtype),
        in_specs=[pl.BlockSpec(memory_space=pltpu.SMEM), pl.BlockSpec(memory_space=pl.ANY)],
        out_specs=pl.BlockSpec(memory_space=pl.ANY),
        scratch_shapes=[
            pltpu.VMEM((chosen, tokens, TILE), y.dtype),
            pltpu.SemaphoreType.DMA((chosen,)),
            pltpu.SemaphoreType.DMA((chosen,)),
        ],
        cost_estimate=pl.CostEstimate(
            flops=0, bytes_accessed=4 * chosen * tokens * TILE, transcendentals=0
        ),
        name="pack_panels",
    )(picks, y)


def square_body(apart, steps_ref, rows_ref, cols_ref, slots_ref, x_ref, y_ref, a_ref, b_ref, keep_ref, send_ref):
    del a_ref, b_ref
    tokens = x_ref.shape[1]
    half = TILE // 2
    first = lax.axis_index("tok") == 0

    def one_slot(x_tile, y_tile, keep_tile, send_tile):
        gradient = lax.dot_general(
            x_tile[0], y_tile[0], (((0,), (0,)), ((), ())), preferred_element_type=jnp.float32
        )
        squares = gradient * gradient

        @pl.when(first)
        def _():
            keep_tile[0] = squares[:half]
            send_tile[0] = squares[half:]

        @pl.when(jnp.logical_not(first))
        def _():
            keep_tile[0] = squares[half:]
            send_tile[0] = squares[:half]

    y_map = (lambda i: (cols_ref[i], 0, 0)) if apart else (lambda i: (0, 0, cols_ref[i]))
    out_spec = pl.BlockSpec((1, half, TILE), lambda i: (slots_ref[i], 0, 0))
    pltpu.emit_pipeline(
        one_slot,
        grid=(steps_ref[0],),
        in_specs=[
            pl.BlockSpec((1, tokens, TILE), lambda i: (0, 0, rows_ref[i])),
            pl.BlockSpec((1, tokens, TILE), y_map),
        ],
        out_specs=[out_spec, out_spec],
    )(x_ref, y_ref, keep_ref, send_ref)


def square_slots(x, y, steps, rows, cols, slots, keep, send, panels_apart):
    tokens = x.shape[1]
    any_spec = pl.BlockSpec(memory_space=pl.ANY)
    smem_spec = pl.BlockSpec(memory_space=pltpu.SMEM)
    expected = max(1, rows.shape[0] // (8 if panels_apart else 2))
    return pl.pallas_call(
        functools.partial(square_body, panels_apart),
        out_shape=(
            jax.ShapeDtypeStruct(keep.shape, keep.dtype),
            jax.ShapeDtypeStruct(send.shape, send.dtype),
        ),
        in_specs=[smem_spec] * 4 + [any_spec] * 4,
        out_specs=(any_spec, any_spec),
        input_output_aliases={6: 0, 7: 1},
        cost_estimate=pl.CostEstimate(
            flops=expected * 2 * tokens * TILE * TILE,
            bytes_accessed=expected * (4 * tokens * TILE + 4 * TILE * TILE),
            transcendentals=0,
        ),
        name="square_slots",
    )(steps.reshape(1), rows, cols, slots, x, y, keep, send)


def chunk_sizes(total):
    last = max(1, total // 8)
    rest = total - last
    parts = 3
    sizes = [rest // parts + (1 if i < rest % parts else 0) for i in range(parts)]
    return sizes + [last]


def phase(x, lists, panels, low, high, keep, send, apart):
    keys, rows, cols, slots = lists
    capacity = rows.shape[0]
    dummy = keep.shape[0] - 1
    begin = jnp.sum((keys < low).astype(jnp.int32))
    steps = jnp.sum((keys < high).astype(jnp.int32)) - begin
    live = steps > 0
    roll = lambda v: lax.dynamic_slice(jnp.concatenate([v, v]), (begin,), (capacity,))
    here_cols = roll(cols) - (low if apart else 0)
    here_cols = jnp.where(live, here_cols, 0)
    here_cols = jnp.clip(here_cols, 0, (high - low - 1) if apart else panels.shape[2] // TILE - 1)
    here_slots = jnp.where(live, roll(slots), dummy)
    return square_slots(
        x, panels, jnp.maximum(steps, 1), roll(rows), here_cols, here_slots, keep, send, apart
    )


def exchange_and_square(total, operands):
    x, y, picks, keys, rows, cols, slots, keep, send = operands
    sizes = chunk_sizes(total)
    swap = [(0, 1), (1, 0)]
    arrived = []
    first = 0
    for size in sizes:
        packed = pack_panels(y, picks[first : first + size])
        arrived.append(lax.ppermute(packed, "rows", swap))
        first += size
    lists = (keys, rows, cols, slots)
    keep, send = phase(x, lists, y, -2, -1, keep, send, False)
    first = 0
    for size, panels in zip(sizes, arrived):
        keep, send = phase(x, lists, panels, first, first + size, keep, send, True)
        first += size
    return keep, send


def on_pair(x_act, grad_out, surv_rows, surv_cols, counts):
    own_tiles = grad_out.shape[2] // TILE
    early = lax.ppermute(grad_out[:, :, : HEAD * TILE], "rows", [(0, 1), (1, 0)])
    capacity = surv_rows.shape[2]
    row_place = lax.axis_index("rows")
    slot_ids = jnp.arange(capacity, dtype=jnp.int32)
    live = slot_ids < counts[0, 0]
    listed = jnp.where(live, surv_cols[0, 0], -1)
    everyone = share_lists(listed)
    columns = jnp.arange(2 * own_tiles, dtype=jnp.int32)
    needed = jnp.any(everyone[:, None, :] == columns[None, :, None], axis=2)
    owner_rows = (jnp.arange(everyone.shape[0], dtype=jnp.int32) % 2)[:, None]
    remote = needed & ((columns // own_tiles)[None, :] != owner_rows)
    remote = remote & (columns % own_tiles >= HEAD)[None, :]
    largest = jnp.max(jnp.sum(remote.astype(jnp.int32), axis=1))

    me = (lax.axis_index("groups") * lax.axis_size("tiles") + lax.axis_index("tiles")) * 2 + row_place

    def places(owner, holder):
        wanted = lax.dynamic_slice(remote, (owner, holder * own_tiles), (1, own_tiles))[0]
        wanted = wanted.astype(jnp.int32)
        ids = jnp.arange(own_tiles, dtype=jnp.int32)
        before = jnp.sum(jnp.where(ids[None, :] < ids[:, None], wanted[None, :], 0), axis=1)
        return wanted, before

    ids = jnp.arange(own_tiles, dtype=jnp.int32)
    partner = me + 1 - 2 * row_place
    wanted, before = places(partner, row_place)
    picks = jnp.sum(
        jnp.where((wanted[None, :] > 0) & (before[None, :] == ids[:, None]), ids[None, :], 0), axis=1
    )
    _, arrival = places(me, 1 - row_place)
    within = listed % own_tiles
    is_local = listed // own_tiles == row_place
    place = jnp.sum(jnp.where(within[:, None] == ids[None, :], arrival[None, :], 0), axis=1)
    is_early = ~is_local & (within < HEAD)
    key = jnp.where(is_local, -2, jnp.where(is_early, -1, place))
    key = jnp.where(live, key, 2 * own_tiles)
    ahead = (key[None, :] < key[:, None]) | (
        (key[None, :] == key[:, None]) & (slot_ids[None, :] < slot_ids[:, None])
    )
    rank = jnp.sum(ahead.astype(jnp.int32), axis=1)
    chosen = rank[None, :] == slot_ids[:, None]
    ordered = lambda v: jnp.sum(jnp.where(chosen, v[None, :], 0), axis=1)
    keys = ordered(key)
    rows = ordered(surv_rows[0, 0])
    cols = ordered(jnp.where(is_local | is_early, within, place))
    slots = ordered(slot_ids)

    half = TILE // 2
    keep = jnp.zeros((capacity + 1, half, TILE), jnp.float32)
    send = jnp.zeros((capacity + 1, half, TILE), jnp.float32)
    totals = sorted({max(4, own_tiles * n // 28) for n in TOTALS} | {own_tiles})
    branch = jnp.sum((largest > jnp.array(totals[:-1], jnp.int32)).astype(jnp.int32))
    operands = (x_act, grad_out, picks, keys, rows, cols, slots, keep, send)
    keep, send = lax.switch(
        branch, [functools.partial(exchange_and_square, total) for total in totals], operands
    )
    lists = (keys, rows, cols, slots)
    keep, send = phase(x_act, lists, early, -1, 0, keep, send, False)
    other = lax.ppermute(send, "tok", [(0, 1), (1, 0)])
    return (keep + other)[:capacity][None, None]


HEAD = 4
TOTALS = (8, 10, 12, 13, 14, 15, 16, 17, 18, 19, 20, 22)


def solution(mesh):
    return functools.partial(choose, mesh)


def choose(mesh, x_act, grad_out, surv_rows, surv_cols, counts):
    own_columns = grad_out.shape[2] // (mesh.shape["tiles"] * mesh.shape["rows"])
    paired = (
        mesh.shape["rows"] == 2
        and mesh.shape["tok"] == 2
        and own_columns % TILE == 0
        and own_columns // TILE >= 4
    )
    return spread(mesh, on_pair if paired else on_device)(
        x_act, grad_out, surv_rows, surv_cols, counts
    )


def spread(mesh, body):
    return jax.shard_map(
        body,
        mesh=mesh,
        in_specs=(
            P("tok", "groups", "rows"),
            P("tok", "groups", ("tiles", "rows")),
            P(("groups", "tiles"), "rows", None),
            P(("groups", "tiles"), "rows", None),
            P(("groups", "tiles"), "rows"),
        ),
        out_specs=P(("groups", "tiles"), "rows", None, "tok", None),
        check_vma=False,
    )
```
